32 devices in a mesh: tau: 2 (over x), blk: 16 (over z, y, core).
Axes of the slice: x: 2, y: 2, z: 4, core: 2. Of those that a mesh axis runs over, the one named last changes fastest.
Arguments:
- three_center: bfloat16 [16, 128, 128, 128], P('blk'), may hold values from -0.59765625 to 0.59765625
- green_blocks: bfloat16 [2, 128, 2048], P('tau', 'blk'), may hold values from -0.5 to 0.5
- block_owner: int32 [768], P('blk'), may hold values from 0 to 15, as said below
- block_slot: int32 [768], P('blk'), may hold values from 0 to 7
- fold_weights: float32 [2, 2], P(None, 'tau'), may hold values from -1 to 1
Outputs:
- chi_freq: float32 [2, 2048, 384], P('tau', 'blk')
The draws below stay inside these ranges and needn't reach their ends.
Inputs may be any that keep to these rules, and one draw needn't show every extreme that they name: `block_owner`: among the 48 entries of each auxiliary block, no owner appears more than 6 times, and one owner appears exactly 6 times in the entries of every auxiliary block.
All inputs are finite; a program needn't handle non-finite values.
Results may differ from the reference program's by a relative error of at most 0.0041.
Values may be sent and summed in bfloat16 or wider, within the bound.
A program may use at most 128 MiB of HBM per device.

```python
import jax
import jax.numpy as jnp
from jax import lax

AB = 32
NS = 4
AUXB = 128
HALF = 1
G_DEV = 8
RW = 128
NPART = 3
NREQ = 48
NAUXB = 16
NAUX = 2048
NTAU = 2
NFREQ = 2
GBLOCKS = 128
CAP = 6


def draw_block_owner(key, part):
    busiest = jax.random.randint(jax.random.fold_in(key, 7919), (), 0, NAUXB).astype(jnp.int32)

    def device_owners(device_index):
        device_key = jax.random.fold_in(key, device_index)
        others = jax.random.permutation(jax.random.fold_in(device_key, 1), NAUXB - 1).astype(jnp.int32)
        row_index = jnp.arange(NREQ - CAP, dtype=jnp.int32)
        other_owner = others[row_index % (NAUXB - 1)]
        other_owner = other_owner + (other_owner >= busiest).astype(jnp.int32)
        assigned = jnp.concatenate([jnp.full((CAP,), busiest, dtype=jnp.int32), other_owner])
        shuffle = jax.random.permutation(jax.random.fold_in(device_key, 2), NREQ)
        return assigned[shuffle]
    owners = jax.vmap(device_owners)(jnp.arange(NAUXB, dtype=jnp.int32))
    return owners.reshape(-1).astype(jnp.int32)


def touch_ends(drawn, stream_key, smallest, top_value):
    extent = drawn.shape
    place = [jax.random.randint(jax.random.fold_in(stream_key, axis), (), 0, extent[axis]) for axis in range(len(extent))]
    drawn = drawn.at[tuple(place)].set(smallest)
    longest = extent.index(max(extent))
    place[longest] = (place[longest] + 1) % extent[longest]
    return drawn.at[tuple(place)].set(top_value)


def steps_of(own_key, dims, cuts, smallest, largest):
    loudness = 1.0
    for axis_at, blocks in cuts:
        draws = jax.random.uniform(jax.random.fold_in(jax.random.fold_in(own_key, 6), axis_at), (blocks,), jnp.float32, smallest / len(cuts), largest / len(cuts))
        loudness = loudness * jnp.repeat(jnp.exp(draws), dims[axis_at] // blocks).reshape((-1,) + (1,) * (len(dims) - 1 - axis_at))
    return loudness


def normal_values(stream_key, dims, width, bound, shards=(), kind=jnp.bfloat16):
    loudness = steps_of(stream_key, dims, shards, -0.22, 0.18) if shards else 1.0
    entries = jax.random.normal(stream_key, dims, jnp.float32) * width * loudness
    return jnp.minimum(jnp.maximum(entries, -bound), bound).astype(kind)


def setup_inputs(seed: int = 0) -> dict:
    keys = jax.random.split(jax.random.key(seed), 6)
    return {
        "three_center": normal_values(keys[0], (NAUXB, RW, RW, AUXB), 0.1, 0.59765625, ((0, 16),)),
        "green_blocks": normal_values(keys[1], (NTAU, GBLOCKS, 2 * AB * AB), RW ** -0.5, 0.5, ((0, 2), (1, 16))),
        "block_owner": draw_block_owner(jax.random.fold_in(keys[5], 71), 0),
        "block_slot": touch_ends(jax.random.randint(keys[3], (NAUXB * NREQ,), 0, G_DEV), jax.random.fold_in(keys[3], 1), 0, G_DEV - 1).astype(jnp.int32),
        "fold_weights": jnp.clip(jax.random.uniform(keys[4], (NFREQ, NTAU), jnp.float32, -1.0, 1.0) * steps_of(keys[4], (NFREQ, NTAU), ((1, 2),), -0.4, 0.0), -1.0, 1.0),
    }


def green_pair(local_table, index_grid):
    blocks = jnp.take(local_table, index_grid.reshape(-1), axis=0)
    blocks = blocks.reshape(NS, NS, 2, AB, AB)
    occupied = blocks[:, :, 0].transpose(0, 2, 1, 3).reshape(NS * AB, NS * AB)
    virtual = blocks[:, :, 1].transpose(0, 2, 1, 3).reshape(NS * AB, NS * AB)
    return occupied, virtual


def transform(occupied, virtual, source):
    region = source.shape[0]
    aux_width = source.shape[2]
    halfway = jnp.einsum("sn,mnb->msb", virtual.astype(jnp.float32), source.astype(jnp.float32)).astype(jnp.bfloat16)
    image_block = jnp.dot(occupied, halfway.reshape(region, region * aux_width), preferred_element_type=jnp.float32)
    return image_block.astype(jnp.bfloat16).reshape(region, region, aux_width)


def pair_block(partner, image_block):
    region = partner.shape[0]
    aux_width = partner.shape[2]
    flat_image = image_block.reshape(region * region, aux_width)
    flat_partner = partner.reshape(region * region, aux_width)
    return -2.0 * jnp.dot(flat_image.T, flat_partner, preferred_element_type=jnp.float32)


def reference(three_center, green_blocks, block_owner, block_slot, fold_weights):
    block_ids = (block_owner * G_DEV + block_slot).astype(jnp.int32).reshape(NAUXB, NPART, NS, NS)

    def column(aux_index):
        source = lax.dynamic_index_in_dim(three_center, aux_index, 0, keepdims=False)
        own_ids = lax.dynamic_index_in_dim(block_ids, aux_index, 0, keepdims=False)
        per_time = []
        for time_index in range(NTAU):
            local_table = green_blocks[time_index]
            pieces = []
            for slot_index in range(NPART):
                occupied, virtual = green_pair(local_table, own_ids[slot_index])
                image_block = transform(occupied, virtual, source)
                partner_index = ((aux_index + slot_index - HALF) % NAUXB).astype(jnp.int32)
                partner = lax.dynamic_index_in_dim(three_center, partner_index, 0, keepdims=False)
                pieces.append(pair_block(partner, image_block))
            per_time.append(jnp.concatenate(pieces, axis=1))
        return jnp.stack(per_time)

    chi_blocks = lax.map(column, jnp.arange(NAUXB, dtype=jnp.int32))
    folded = jnp.einsum("kt,rtbc->krbc", fold_weights, chi_blocks, precision=lax.Precision.HIGHEST)
    return folded.reshape(NFREQ, NAUX, NPART * AUXB)
```

```python
import jax
import jax.numpy as jnp
from jax import lax
from jax.sharding import PartitionSpec as P

AB = 32
NS = 4
HALF = 1


def green_pairs(blocks):
    count = blocks.shape[0] // (NS * NS)
    blocks = blocks.reshape(count, NS, NS, 2, AB, AB).transpose(3, 0, 1, 4, 2, 5)
    return blocks.reshape(2, count, NS * AB, NS * AB)


def transform(left, right, source):
    halfway = jnp.einsum("sn,mnb->smb", right, source, preferred_element_type=jnp.float32).astype(
        jnp.bfloat16
    )
    return jnp.einsum("lm,smb->slb", left, halfway, preferred_element_type=jnp.float32).astype(
        jnp.bfloat16
    )


def contract(first, second):
    width = first.shape[2]
    return lax.dot_general(
        first.reshape(-1, width),
        second.reshape(-1, width),
        (((0,), (0,)), ((), ())),
        preferred_element_type=jnp.float32,
    )


def exchange(chi, weights, step):
    taus = lax.axis_size("tau")
    blks = lax.axis_size("blk")
    t = lax.axis_index("tau")
    total = None
    for shift in range(taus):
        target = lax.rem(t + shift, taus)
        piece = lax.dynamic_index_in_dim(weights, target, 0, keepdims=False) * chi
        if shift or step:
            perm = [
                (i * blks + j, ((i + shift) % taus) * blks + (j + step) % blks)
                for i in range(taus)
                for j in range(blks)
            ]
            piece = lax.ppermute(piece, ("tau", "blk"), perm)
        total = piece if total is None else total + piece
    return total


def local(three_center, green_blocks, block_owner, block_slot, fold_weights):
    source = three_center[0]
    devices = lax.axis_size("blk")
    per_slot = NS * NS
    ahead = [(i, (i - 1) % devices) for i in range(devices)]
    ids = block_owner * green_blocks.shape[1] + block_slot
    table = lax.all_gather(green_blocks[0], "blk", axis=0, tiled=True)
    next_ids = lax.ppermute(ids[:per_slot], "blk", ahead)
    used = jnp.concatenate([next_ids, ids[per_slot:]])
    fetched = table.at[used].get(mode="promise_in_bounds")
    flipped = source.transpose(1, 0, 2)
    partner = lax.ppermute(flipped, "blk", ahead)
    occupied, virtual = green_pairs(fetched)
    weights = fold_weights[:, 0] * -2.0
    own = transform(occupied[1], virtual[1], source)
    down = transform(occupied[0].T, virtual[0].T, source)
    up = transform(occupied[2], virtual[2], source)
    out_own = exchange(contract(own, flipped), weights, 0)
    out_down = exchange(contract(partner, down), weights, 1)
    out_up = exchange(contract(up, partner), weights, 0)
    return jnp.concatenate([out_down, out_own, out_up], axis=1)[None]


def solution(mesh):
    return jax.shard_map(
        local,
        mesh=mesh,
        in_specs=(
            P("blk", None, None, None),
            P("tau", "blk", None),
            P("blk"),
            P("blk"),
            P(None, "tau"),
        ),
        out_specs=P("tau", "blk", None),
        check_vma=False,
    )
```

```python
import jax
import jax.numpy as jnp
from jax import lax
from jax.sharding import PartitionSpec as P

AB = 32
NS = 4
CHUNKS = 2


def green_pairs(blocks):
    count = blocks.shape[0] // (NS * NS)
    blocks = blocks.reshape(count, NS, NS, 2, AB, AB).transpose(3, 0, 1, 4, 2, 5)
    return blocks.reshape(2, count, NS * AB, NS * AB)


def transform(left, right, source):
    halfway = jnp.einsum("sn,mnb->smb", right, source, preferred_element_type=jnp.float32).astype(
        jnp.bfloat16
    )
    return jnp.einsum("lm,smb->slb", left, halfway, preferred_element_type=jnp.float32).astype(
        jnp.bfloat16
    )


def contract(first, second):
    width = first.shape[2]
    return lax.dot_general(
        first.reshape(-1, width),
        second.reshape(-1, width),
        (((0,), (0,)), ((), ())),
        preferred_element_type=jnp.float32,
    )


def exchange(chi, weights, step):
    taus = lax.axis_size("tau")
    blks = lax.axis_size("blk")
    t = lax.axis_index("tau")
    total = None
    for shift in range(taus):
        target = lax.rem(t + shift, taus)
        piece = lax.dynamic_index_in_dim(weights, target, 0, keepdims=False) * chi
        if shift or step:
            perm = [
                (i * blks + j, ((i + shift) % taus) * blks + (j + step) % blks)
                for i in range(taus)
                for j in range(blks)
            ]
            piece = lax.ppermute(piece, ("tau", "blk"), perm)
        total = piece if total is None else total + piece
    return total


def pull_ahead(value):
    taus = lax.axis_size("tau")
    blks = lax.axis_size("blk")
    rows = value.shape[0]
    if taus != 2 or blks % 2 or rows % (2 * CHUNKS):
        whole = lax.ppermute(value, "blk", [(i, (i - 1) % blks) for i in range(blks)])
        return [(0, whole)]
    t = lax.axis_index("tau")
    odd = lax.axis_index("blk") % 2 == 1
    half = rows // 2
    step = half // CHUNKS
    mine, other = t * half, (1 - t) * half
    evens = [(i, (i - 1) % blks) for i in range(0, blks, 2)]
    odds = [(i, i - 1) for i in range(1, blks, 2)]
    swap = [(i * blks + j, (1 - i) * blks + j) for i in range(2) for j in range(1, blks, 2)]
    near, far = [], []
    for k in range(CHUNKS):
        part = lax.dynamic_slice_in_dim(value, mine + k * step, step, 0)
        near.append(lax.ppermute(part, "blk", evens))
    whole = lax.ppermute(value, "blk", odds)
    for part in near:
        far.append(lax.ppermute(part, ("tau", "blk"), swap))
    first = jnp.where(odd, jnp.concatenate(near), lax.dynamic_slice_in_dim(whole, mine, half, 0))
    second = jnp.where(odd, jnp.concatenate(far), lax.dynamic_slice_in_dim(whole, other, half, 0))
    return [(mine, first), (other, second)]


def local(three_center, green_blocks, block_owner, block_slot, fold_weights):
    source = three_center[0]
    devices = lax.axis_size("blk")
    per_slot = NS * NS
    ids = block_owner * green_blocks.shape[1] + block_slot
    next_ids = lax.ppermute(ids[:per_slot], "blk", [(i, (i - 1) % devices) for i in range(devices)])
    table = lax.all_gather(green_blocks[0], "blk", axis=0, tiled=True)
    used = jnp.concatenate([next_ids, ids[per_slot:]])
    flipped = source.transpose(1, 0, 2)
    table, used, sent = lax.optimization_barrier((table, used, flipped))
    halves = pull_ahead(sent)
    fetched = table.at[used].get(mode="promise_in_bounds")
    occupied, virtual = green_pairs(fetched)
    weights = fold_weights[:, 0] * -2.0
    own = transform(occupied[1], virtual[1], source)
    out_own = exchange(contract(own, flipped), weights, 0)
    down = transform(occupied[0].T, virtual[0].T, source)
    up = transform(occupied[2], virtual[2], source)
    down, up = lax.optimization_barrier((down, up))
    chi_down = chi_up = 0.0
    for start, half in halves:
        rows = half.shape[0]
        chi_down += contract(half, lax.dynamic_slice_in_dim(down, start, rows, 0))
        chi_up += contract(lax.dynamic_slice_in_dim(up, start, rows, 0), half)
    out_down = exchange(chi_down, weights, 1)
    out_up = exchange(chi_up, weights, 0)
    return jnp.concatenate([out_down, out_own, out_up], axis=1)[None]


def solution(mesh):
    return jax.shard_map(
        local,
        mesh=mesh,
        in_specs=(
            P("blk", None, None, None),
            P("tau", "blk", None),
            P("blk"),
            P("blk"),
            P(None, "tau"),
        ),
        out_specs=P("tau", "blk", None),
        check_vma=False,
    )
```

```python
import functools

import jax
import jax.numpy as jnp
from jax import lax
from jax.experimental import pallas as pl
from jax.experimental.pallas import tpu as pltpu
from jax.sharding import PartitionSpec as P

AB = 32
NS = 4
CHUNKS = 2


def green_pairs(blocks):
    count = blocks.shape[0] // (NS * NS)
    blocks = blocks.reshape(count, NS, NS, 2, AB, AB).transpose(3, 0, 1, 4, 2, 5)
    return blocks.reshape(2, count, NS * AB, NS * AB)


GROUP = 4


def transform_kernel(occupied, virtual, source, own, down, up, flipped, first):
    region = source.shape[0]

    def flip(g, _):
        for k in range(GROUP):
            m = g * GROUP + k
            flipped[pl.ds(m, region, stride=region), :] = source[m].astype(jnp.float32)
        return 0

    lax.fori_loop(0, region // GROUP, flip, 0)

    def left(g, _):
        for k in range(GROUP):
            n = g * GROUP + k
            block = flipped[pl.ds(pl.multiple_of(n * region, region), region), :].astype(jnp.bfloat16)
            product = jnp.dot(occupied[...], block, preferred_element_type=jnp.float32)
            for j in range(3):
                first[j, pl.ds(n, region, stride=region), :] = product[j * region : (j + 1) * region]
        return 0

    lax.fori_loop(0, region // GROUP, left, 0)
    own[...] = jnp.zeros_like(own)

    def right(g, _):
        images = []
        for k in range(GROUP):
            l = g * GROUP + k
            for j, out in enumerate((down, None, up)):
                block = first[j, pl.ds(pl.multiple_of(l * region, region), region), :]
                image = jnp.dot(
                    virtual[j], block.astype(jnp.bfloat16), preferred_element_type=jnp.float32
                ).astype(jnp.bfloat16)
                if out is None:
                    images.append(image)
                else:
                    out[l] = image
        own[...] += lax.dot_general(
            jnp.concatenate(images, axis=0),
            source[pl.ds(g * GROUP, GROUP)].reshape(GROUP * region, -1),
            (((0,), (0,)), ((), ())),
            preferred_element_type=jnp.float32,
        )
        return 0

    lax.fori_loop(0, region // GROUP, right, 0)


def transform(occupied, virtual, source):
    region, _, width = source.shape
    vmem = pl.BlockSpec(memory_space=pltpu.VMEM)
    image = jax.ShapeDtypeStruct((region, region, width), jnp.bfloat16)
    return pl.pallas_call(
        transform_kernel,
        out_shape=(jax.ShapeDtypeStruct((width, width), jnp.float32), image, image),
        in_specs=[vmem] * 3,
        out_specs=(vmem,) * 3,
        scratch_shapes=[
            pltpu.VMEM((region * region, width), jnp.float32),
            pltpu.VMEM((3, region * region, width), jnp.float32),
        ],
        compiler_params=pltpu.CompilerParams(vmem_limit_bytes=56 * 2**20),
        cost_estimate=pl.CostEstimate(
            flops=2 * 7 * region**3 * width, bytes_accessed=12 * 2**20, transcendentals=0
        ),
        name="transform",
    )(occupied.reshape(3 * region, region), virtual, source)


def contract_kernel(pieces, *refs):
    down, up = refs[:2]
    parts = refs[2 : 2 + pieces]
    chi_down, chi_up, held, sem = refs[2 + pieces :]
    region = held.shape[0]

    def bring(source, start):
        copy = pltpu.make_async_copy(source, held.at[pl.ds(start, source.shape[0])], sem)
        copy.start()
        return copy

    if pieces == 1:
        bring(parts[0], 0).wait()
    else:
        t = lax.axis_index("tau")
        odd = lax.axis_index("blk") % 2
        step = parts[1].shape[0]

        @pl.when(odd == 0)
        def _():
            bring(parts[0], 0).wait()

        @pl.when(odd == 1)
        def _():
            for side in range(2):
                start = (t if side == 0 else 1 - t) * (region // 2)
                for k in range(CHUNKS):
                    bring(parts[1 + side * CHUNKS + k], start + k * step).wait()

    chi_down[...] = jnp.zeros_like(chi_down)
    chi_up[...] = jnp.zeros_like(chi_up)
    width = held.shape[2]
    rows = 8

    def body(g, _):
        def flat(ref):
            return ref[pl.ds(g * rows, rows)].reshape(rows * region, width)

        partner = flat(held)
        dims = (((0,), (0,)), ((), ()))
        chi_down[...] += lax.dot_general(partner, flat(down), dims, preferred_element_type=jnp.float32)
        chi_up[...] += lax.dot_general(flat(up), partner, dims, preferred_element_type=jnp.float32)
        return 0

    lax.fori_loop(0, region // rows, body, 0)


def contract(down, up, parts):
    region, _, width = down.shape
    vmem = pl.BlockSpec(memory_space=pltpu.VMEM)
    anywhere = pl.BlockSpec(memory_space=pl.ANY)
    chi = jax.ShapeDtypeStruct((width, width), jnp.float32)
    return pl.pallas_call(
        functools.partial(contract_kernel, len(parts)),
        out_shape=(chi, chi),
        in_specs=[vmem] * 2 + [anywhere] * len(parts),
        out_specs=(vmem, vmem),
        scratch_shapes=[pltpu.VMEM((region, region, width), jnp.bfloat16), pltpu.SemaphoreType.DMA],
        compiler_params=pltpu.CompilerParams(vmem_limit_bytes=32 * 2**20),
        cost_estimate=pl.CostEstimate(
            flops=4 * region**2 * width**2, bytes_accessed=12 * 2**20, transcendentals=0
        ),
        name="contract",
    )(down, up, *parts)


def exchange(chi, weights, step):
    taus = lax.axis_size("tau")
    blks = lax.axis_size("blk")
    t = lax.axis_index("tau")
    total = None
    for shift in range(taus):
        target = lax.rem(t + shift, taus)
        piece = lax.dynamic_index_in_dim(weights, target, 0, keepdims=False) * chi
        if shift or step:
            perm = [
                (i * blks + j, ((i + shift) % taus) * blks + (j + step) % blks)
                for i in range(taus)
                for j in range(blks)
            ]
            piece = lax.ppermute(piece, ("tau", "blk"), perm)
        total = piece if total is None else total + piece
    return total


def pull_ahead(value):
    taus = lax.axis_size("tau")
    blks = lax.axis_size("blk")
    rows = value.shape[0]
    if taus != 2 or blks % 2 or rows % (2 * CHUNKS):
        return [lax.ppermute(value, "blk", [(i, (i - 1) % blks) for i in range(blks)])]
    half = rows // 2
    step = half // CHUNKS
    mine = lax.axis_index("tau") * half
    evens = [(i, (i - 1) % blks) for i in range(0, blks, 2)]
    odds = [(i, i - 1) for i in range(1, blks, 2)]
    swap = [(i * blks + j, (1 - i) * blks + j) for i in range(2) for j in range(1, blks, 2)]
    near, far = [], []
    for k in range(CHUNKS):
        part = lax.dynamic_slice_in_dim(value, mine + k * step, step, 0)
        near.append(lax.ppermute(part, "blk", evens))
    whole = lax.ppermute(value, "blk", odds)
    for part in near:
        far.append(lax.ppermute(part, ("tau", "blk"), swap))
    return [whole, *near, *far]


def local(three_center, green_blocks, block_owner, block_slot, fold_weights):
    source = three_center[0]
    devices = lax.axis_size("blk")
    per_slot = NS * NS
    ids = block_owner * green_blocks.shape[1] + block_slot
    next_ids = lax.ppermute(ids[:per_slot], "blk", [(i, (i - 1) % devices) for i in range(devices)])
    table = lax.all_gather(green_blocks[0], "blk", axis=0, tiled=True)
    used = jnp.concatenate([next_ids, ids[per_slot:]])
    table, used, sent = lax.optimization_barrier((table, used, source))
    parts = pull_ahead(sent)
    fetched = table.at[used].get(mode="promise_in_bounds")
    occupied, virtual = green_pairs(fetched)
    occupied = jnp.concatenate([occupied[:1].swapaxes(1, 2), occupied[1:]])
    virtual = jnp.concatenate([virtual[:1].swapaxes(1, 2), virtual[1:]])
    weights = fold_weights[:, 0] * -2.0
    chi_own, down, up = transform(occupied, virtual, source)
    out_own = exchange(chi_own, weights, 0)
    chi_down, chi_up = contract(down, up, parts)
    out_down = exchange(chi_down, weights, 1)
    out_up = exchange(chi_up, weights, 0)
    return jnp.concatenate([out_down, out_own, out_up], axis=1)[None]


def solution(mesh):
    return jax.shard_map(
        local,
        mesh=mesh,
        in_specs=(
            P("blk", None, None, None),
            P("tau", "blk", None),
            P("blk"),
            P("blk"),
            P(None, "tau"),
        ),
        out_specs=P("tau", "blk", None),
        check_vma=False,
    )
```

```python
import functools

import jax
import jax.numpy as jnp
from jax import lax
from jax.experimental import pallas as pl
from jax.experimental.pallas import tpu as pltpu
from jax.sharding import PartitionSpec as P

AB = 32
NS = 4


def green_pairs(blocks):
    count = blocks.shape[0] // (NS * NS)
    blocks = blocks.reshape(count, NS, NS, 2, AB, AB).transpose(3, 0, 1, 4, 2, 5)
    return blocks.reshape(2, count, NS * AB, NS * AB)


def transform_kernel(own_at, occupied, virtual, source, *refs):
    pairs, region = virtual.shape[:2]
    outs, (flipped, first) = list(refs[:-2]), refs[-2:]
    own = outs.pop(own_at) if own_at is not None else None
    group = 16
    few = 8

    def flip(g, _):
        at = pl.ds(pl.multiple_of(g * group, group), group)
        flipped[:, at, :] = jnp.swapaxes(source[at], 0, 1)
        return 0

    lax.fori_loop(0, region // group, flip, 0)

    def left(g, _):
        at = pl.ds(pl.multiple_of(g * group, group), group)
        for j in range(pairs):
            products = [
                jnp.dot(
                    occupied[j], flipped[g * group + k], preferred_element_type=jnp.float32
                ).astype(jnp.bfloat16)
                for k in range(group)
            ]
            first[j, :, at, :] = jnp.swapaxes(jnp.stack(products), 0, 1)
        return 0

    lax.fori_loop(0, region // group, left, 0)
    if own is not None:
        own[...] = jnp.zeros_like(own)

    def right(g, _):
        images = []
        for k in range(few):
            l = g * few + k
            for j in range(pairs):
                image = jnp.dot(
                    virtual[j], first[j, l], preferred_element_type=jnp.float32
                ).astype(jnp.bfloat16)
                if j == own_at:
                    images.append(image)
                else:
                    outs[j - (own_at is not None and j > own_at)][l] = image
        if own is not None:
            own[...] += lax.dot_general(
                jnp.concatenate(images, axis=0),
                source[pl.ds(g * few, few)].reshape(few * region, -1),
                (((0,), (0,)), ((), ())),
                preferred_element_type=jnp.float32,
            )
        return 0

    lax.fori_loop(0, region // few, right, 0)


def transform(occupied, virtual, source, own_at):
    region, _, width = source.shape
    pairs = virtual.shape[0]
    vmem = pl.BlockSpec(memory_space=pltpu.VMEM)
    image = jax.ShapeDtypeStruct((region, region, width), jnp.bfloat16)
    shapes = [image] * pairs
    if own_at is not None:
        shapes[own_at] = jax.ShapeDtypeStruct((width, width), jnp.float32)
    return pl.pallas_call(
        functools.partial(transform_kernel, own_at),
        out_shape=shapes,
        in_specs=[vmem] * 3,
        out_specs=[vmem] * pairs,
        scratch_shapes=[
            pltpu.VMEM((region, region, width), jnp.bfloat16),
            pltpu.VMEM((pairs, region, region, width), jnp.bfloat16),
        ],
        compiler_params=pltpu.CompilerParams(vmem_limit_bytes=40 * 2**20),
        cost_estimate=pl.CostEstimate(
            flops=12 * pairs * region**3 * width, bytes_accessed=8 * 2**20, transcendentals=0
        ),
        name="transform",
    )(occupied, virtual, source)


def contract_kernel(pieces, *refs):
    down, up = refs[:2]
    parts = refs[2 : 2 + pieces]
    chi_down, chi_up, held, sem = refs[2 + pieces :]
    region = held.shape[0]

    def bring(moves):
        copies = [
            pltpu.make_async_copy(source, held.at[pl.ds(start, source.shape[0])], sem.at[i])
            for i, (source, start) in enumerate(moves)
        ]
        for copy in copies:
            copy.start()
        for copy in copies:
            copy.wait()

    if pieces == 1:
        bring([(parts[0], 0)])
    else:
        t = lax.axis_index("tau")
        odd = lax.axis_index("blk") % 2
        step = parts[1].shape[0]

        @pl.when(odd == 0)
        def _():
            bring([(parts[0], 0)])

        @pl.when(odd == 1)
        def _():
            bring([(parts[1], t * (region - step)), (parts[2], step), (parts[3], (1 - t) * (region - step))])

    chi_down[...] = jnp.zeros_like(chi_down)
    chi_up[...] = jnp.zeros_like(chi_up)
    width = held.shape[2]
    rows = 8

    def body(g, _):
        def flat(ref):
            return ref[pl.ds(g * rows, rows)].reshape(rows * region, width)

        partner = flat(held)
        dims = (((0,), (0,)), ((), ()))
        chi_down[...] += lax.dot_general(partner, flat(down), dims, preferred_element_type=jnp.float32)
        chi_up[...] += lax.dot_general(flat(up), partner, dims, preferred_element_type=jnp.float32)
        return 0

    lax.fori_loop(0, region // rows, body, 0)


def contract(down, up, parts):
    region, _, width = down.shape
    vmem = pl.BlockSpec(memory_space=pltpu.VMEM)
    anywhere = pl.BlockSpec(memory_space=pl.ANY)
    chi = jax.ShapeDtypeStruct((width, width), jnp.float32)
    return pl.pallas_call(
        functools.partial(contract_kernel, len(parts)),
        out_shape=(chi, chi),
        in_specs=[vmem] * 2 + [anywhere] * len(parts),
        out_specs=(vmem, vmem),
        scratch_shapes=[pltpu.VMEM((region, region, width), jnp.bfloat16), pltpu.SemaphoreType.DMA((3,))],
        compiler_params=pltpu.CompilerParams(vmem_limit_bytes=32 * 2**20),
        cost_estimate=pl.CostEstimate(
            flops=4 * region**2 * width**2, bytes_accessed=12 * 2**20, transcendentals=0
        ),
        name="contract",
    )(down, up, *parts)


def exchange(chi, weights, step):
    taus = lax.axis_size("tau")
    blks = lax.axis_size("blk")
    t = lax.axis_index("tau")
    total = None
    for shift in range(taus):
        target = lax.rem(t + shift, taus)
        piece = lax.dynamic_index_in_dim(weights, target, 0, keepdims=False) * chi
        if shift or step:
            perm = [
                (i * blks + j, ((i + shift) % taus) * blks + (j + step) % blks)
                for i in range(taus)
                for j in range(blks)
            ]
            piece = lax.ppermute(piece, ("tau", "blk"), perm)
        total = piece if total is None else total + piece
    return total


def pull_ahead(value):
    taus = lax.axis_size("tau")
    blks = lax.axis_size("blk")
    rows = value.shape[0]
    if taus != 2 or blks % 2 or rows % 4:
        return [lax.ppermute(value, "blk", [(i, (i - 1) % blks) for i in range(blks)])]
    quarter = rows // 4
    evens = [(i, (i - 1) % blks) for i in range(0, blks, 2)]
    odds = [(i, i - 1) for i in range(1, blks, 2)]
    start = lax.axis_index("tau") * (rows - quarter)
    end = lax.ppermute(lax.dynamic_slice_in_dim(value, start, quarter, 0), "blk", evens)
    middle = lax.ppermute(value[quarter : rows - quarter], "blk", evens)
    return [lax.ppermute(value, "blk", odds), end, middle]


def swap_planes(end):
    blks = lax.axis_size("blk")
    pairs = [(i * blks + j, (1 - i) * blks + j) for i in range(2) for j in range(1, blks, 2)]
    return lax.ppermute(end, ("tau", "blk"), pairs)


def local(three_center, green_blocks, block_owner, block_slot, fold_weights):
    source = three_center[0]
    devices = lax.axis_size("blk")
    per_slot = NS * NS
    ids = block_owner * green_blocks.shape[1] + block_slot
    next_ids = lax.ppermute(ids[:per_slot], "blk", [(i, (i - 1) % devices) for i in range(devices)])
    table = lax.all_gather(green_blocks[0], "blk", axis=0, tiled=True)
    used = jnp.concatenate([next_ids, ids[per_slot:]])
    table, used, sent = lax.optimization_barrier((table, used, source))
    parts = pull_ahead(sent)
    fetched = table.at[used].get(mode="promise_in_bounds")
    occupied, virtual = green_pairs(fetched)
    weights = fold_weights[:, 0] * -2.0
    (down,) = transform(occupied[:1].swapaxes(1, 2), virtual[:1].swapaxes(1, 2), source, None)
    occupied, virtual = occupied[1:], virtual[1:]
    if len(parts) > 1:
        down, occupied, virtual, parts[1] = lax.optimization_barrier((down, occupied, virtual, parts[1]))
        parts.append(swap_planes(parts[1]))
    chi_own, up = transform(occupied, virtual, source, 0)
    out_own = exchange(chi_own, weights, 0)
    chi_down, chi_up = contract(down, up, parts)
    out_down = exchange(chi_down, weights, 1)
    out_up = exchange(chi_up, weights, 0)
    return jnp.concatenate([out_down, out_own, out_up], axis=1)[None]


def solution(mesh):
    return jax.shard_map(
        local,
        mesh=mesh,
        in_specs=(
            P("blk", None, None, None),
            P("tau", "blk", None),
            P("blk"),
            P("blk"),
            P(None, "tau"),
        ),
        out_specs=P("tau", "blk", None),
        check_vma=False,
    )
```

```python
import functools

import jax
import jax.numpy as jnp
from jax import lax
from jax.experimental import pallas as pl
from jax.experimental.pallas import tpu as pltpu
from jax.sharding import PartitionSpec as P

AB = 32
NS = 4
LANES = 128


def green_pairs(blocks):
    count = blocks.shape[0] // (NS * NS)
    blocks = blocks.reshape(count, NS, NS, 2, AB, AB).transpose(3, 0, 1, 4, 2, 5)
    return blocks.reshape(2, count, NS * AB, NS * AB)


def transform_kernel(own_at, occupied, virtual, source, *refs):
    pairs, region = virtual.shape[:2]
    outs, (flipped, first) = list(refs[:-2]), refs[-2:]
    own = outs.pop(own_at) if own_at is not None else None
    group = 16
    few = 8

    def flip(g, _):
        at = pl.ds(pl.multiple_of(g * group, group), group)
        flipped[:, at, :] = jnp.swapaxes(source[at], 0, 1)
        return 0

    lax.fori_loop(0, region // group, flip, 0)

    def left(g, _):
        at = pl.ds(pl.multiple_of(g * group, group), group)
        for j in range(pairs):
            products = [
                jnp.dot(
                    occupied[j], flipped[g * group + k], preferred_element_type=jnp.float32
                ).astype(jnp.bfloat16)
                for k in range(group)
            ]
            first[j, :, at, :] = jnp.swapaxes(jnp.stack(products), 0, 1)
        return 0

    lax.fori_loop(0, region // group, left, 0)
    if own is not None:
        own[...] = jnp.zeros_like(own)

    def right(g, _):
        images = []
        for k in range(few):
            l = g * few + k
            for j in range(pairs):
                image = jnp.dot(
                    virtual[j], first[j, l], preferred_element_type=jnp.float32
                ).astype(jnp.bfloat16)
                if j == own_at:
                    images.append(image)
                else:
                    outs[j - (own_at is not None and j > own_at)][l] = image
        if own is not None:
            own[...] += lax.dot_general(
                jnp.concatenate(images, axis=0),
                source[pl.ds(g * few, few)].reshape(few * region, -1),
                (((0,), (0,)), ((), ())),
                preferred_element_type=jnp.float32,
            )
        return 0

    lax.fori_loop(0, region // few, right, 0)


def transform(occupied, virtual, source, own_at):
    region, _, width = source.shape
    pairs = virtual.shape[0]
    vmem = pl.BlockSpec(memory_space=pltpu.VMEM)
    image = jax.ShapeDtypeStruct((region, region, width), jnp.bfloat16)
    shapes = [image] * pairs
    if own_at is not None:
        shapes[own_at] = jax.ShapeDtypeStruct((width, width), jnp.float32)
    return pl.pallas_call(
        functools.partial(transform_kernel, own_at),
        out_shape=shapes,
        in_specs=[vmem] * 3,
        out_specs=[vmem] * pairs,
        scratch_shapes=[
            pltpu.VMEM((region, region, width), jnp.bfloat16),
            pltpu.VMEM((pairs, region, region, width), jnp.bfloat16),
        ],
        compiler_params=pltpu.CompilerParams(vmem_limit_bytes=40 * 2**20),
        cost_estimate=pl.CostEstimate(
            flops=12 * pairs * region**3 * width, bytes_accessed=8 * 2**20, transcendentals=0
        ),
        name="transform",
    )(occupied, virtual, source)


def contract_kernel(pieces, *refs):
    down, up = refs[:2]
    parts = refs[2 : 2 + pieces]
    chi_down, chi_up, held, sem = refs[2 + pieces :]
    region = held.shape[0]

    def bring(moves):
        copies = [
            pltpu.make_async_copy(source, held.at[pl.ds(start, source.shape[0])], sem.at[i])
            for i, (source, start) in enumerate(moves)
        ]
        for copy in copies:
            copy.start()
        for copy in copies:
            copy.wait()

    if pieces == 1:
        bring([(parts[0], 0)])
    else:
        t = lax.axis_index("tau")
        odd = lax.axis_index("blk") % 2
        step = parts[1].shape[0]

        @pl.when(odd == 0)
        def _():
            bring([(parts[0], 0)])

        @pl.when(odd == 1)
        def _():
            bring([(parts[1], t * (region - step)), (parts[2], step), (parts[3], (1 - t) * (region - step))])

    chi_down[...] = jnp.zeros_like(chi_down)
    chi_up[...] = jnp.zeros_like(chi_up)
    width = held.shape[2]
    rows = 8

    def body(g, _):
        def flat(ref):
            return ref[pl.ds(g * rows, rows)].reshape(rows * region, width)

        partner = flat(held)
        dims = (((0,), (0,)), ((), ()))
        chi_down[...] += lax.dot_general(partner, flat(down), dims, preferred_element_type=jnp.float32)
        chi_up[...] += lax.dot_general(flat(up), partner, dims, preferred_element_type=jnp.float32)
        return 0

    lax.fori_loop(0, region // rows, body, 0)


def contract(down, up, parts):
    region, _, width = down.shape
    vmem = pl.BlockSpec(memory_space=pltpu.VMEM)
    anywhere = pl.BlockSpec(memory_space=pl.ANY)
    chi = jax.ShapeDtypeStruct((width, width), jnp.float32)
    return pl.pallas_call(
        functools.partial(contract_kernel, len(parts)),
        out_shape=(chi, chi),
        in_specs=[vmem] * 2 + [anywhere] * len(parts),
        out_specs=(vmem, vmem),
        scratch_shapes=[pltpu.VMEM((region, region, width), jnp.bfloat16), pltpu.SemaphoreType.DMA((3,))],
        compiler_params=pltpu.CompilerParams(vmem_limit_bytes=32 * 2**20),
        cost_estimate=pl.CostEstimate(
            flops=4 * region**2 * width**2, bytes_accessed=12 * 2**20, transcendentals=0
        ),
        name="contract",
    )(down, up, *parts)


def exchange(chi, weights, step):
    taus = lax.axis_size("tau")
    blks = lax.axis_size("blk")
    t = lax.axis_index("tau")
    pieces = []
    for shift in range(taus):
        target = lax.rem(t + shift, taus)
        piece = lax.dynamic_index_in_dim(weights, target, 0, keepdims=False) * chi
        if shift or step:
            perm = [
                (i * blks + j, ((i + shift) % taus) * blks + (j + step) % blks)
                for i in range(taus)
                for j in range(blks)
            ]
            piece = lax.ppermute(piece, ("tau", "blk"), perm)
        pieces.append(piece)
    return pieces


def pull_ahead(value):
    taus = lax.axis_size("tau")
    blks = lax.axis_size("blk")
    rows = value.shape[0]
    if taus != 2 or blks % 2 or rows % 4:
        return [lax.ppermute(value, "blk", [(i, (i - 1) % blks) for i in range(blks)])]
    quarter = rows // 4
    evens = [(i, (i - 1) % blks) for i in range(0, blks, 2)]
    odds = [(i, i - 1) for i in range(1, blks, 2)]
    start = lax.axis_index("tau") * (rows - quarter)
    end = lax.ppermute(lax.dynamic_slice_in_dim(value, start, quarter, 0), "blk", evens)
    middle = lax.ppermute(value[quarter : rows - quarter], "blk", evens)
    return [lax.ppermute(value, "blk", odds), end, middle]


def swap_planes(end):
    blks = lax.axis_size("blk")
    pairs = [(i * blks + j, (1 - i) * blks + j) for i in range(2) for j in range(1, blks, 2)]
    return lax.ppermute(end, ("tau", "blk"), pairs)


def local(three_center, green_blocks, block_owner, block_slot, fold_weights):
    source = three_center[0]
    devices = lax.axis_size("blk")
    per_slot = NS * NS
    slots, length = green_blocks.shape[1:]
    ids = block_owner * slots + block_slot
    asked = jnp.concatenate([block_owner[:per_slot], block_slot[:per_slot]]).astype(jnp.bfloat16)
    riders = jnp.broadcast_to(jnp.pad(asked, (0, LANES - 2 * per_slot)), (slots, LANES))
    table = lax.all_gather(
        jnp.concatenate([green_blocks[0], riders], axis=1), "blk", axis=0, tiled=True
    )
    table, sent = lax.optimization_barrier((table, source))
    ahead = lax.rem(lax.axis_index("blk") + 1, devices)
    asked = lax.dynamic_slice(table, (ahead * slots, length), (1, 2 * per_slot))[0].astype(jnp.int32)
    next_ids = asked[:per_slot] * slots + asked[per_slot:]
    used = jnp.concatenate([next_ids, ids[per_slot:]])
    parts = pull_ahead(sent)
    fetched = table.at[used].get(mode="promise_in_bounds")[:, :length]
    occupied, virtual = green_pairs(fetched)
    weights = fold_weights[:, 0] * -2.0
    (down,) = transform(occupied[:1].swapaxes(1, 2), virtual[:1].swapaxes(1, 2), source, None)
    occupied, virtual = occupied[1:], virtual[1:]
    if len(parts) > 1:
        down, occupied, virtual, parts[1] = lax.optimization_barrier((down, occupied, virtual, parts[1]))
        parts.append(swap_planes(parts[1]))
    chi_own, up = transform(occupied, virtual, source, 0)
    own = exchange(chi_own, weights, 0)
    chi_down, chi_up = contract(down, up, parts)
    chi_down, chi_up, own = lax.optimization_barrier((chi_down, chi_up, own))
    down = exchange(chi_down, weights, 1)
    up = exchange(chi_up, weights, 0)
    return jnp.concatenate([sum(down), sum(own), sum(up)], axis=1)[None]


def solution(mesh):
    return jax.shard_map(
        local,
        mesh=mesh,
        in_specs=(
            P("blk", None, None, None),
            P("tau", "blk", None),
            P("blk"),
            P("blk"),
            P(None, "tau"),
        ),
        out_specs=P("tau", "blk", None),
        check_vma=False,
    )
```

```python
import functools

import jax
import jax.numpy as jnp
from jax import lax
from jax.experimental import pallas as pl
from jax.experimental.pallas import tpu as pltpu
from jax.sharding import PartitionSpec as P

AB = 32
NS = 4
LANES = 128


def green_pairs(blocks):
    count = blocks.shape[0] // (NS * NS)
    blocks = blocks.reshape(count, NS, NS, 2, AB, AB).transpose(3, 0, 1, 4, 2, 5)
    return blocks.reshape(2, count, NS * AB, NS * AB)


def transform_kernel(own_at, occupied, virtual, source, *refs):
    pairs, region = virtual.shape[:2]
    outs, (flipped, first) = list(refs[:-2]), refs[-2:]
    own = outs.pop(own_at) if own_at is not None else None
    group = 16
    few = 8

    def flip(g, _):
        at = pl.ds(pl.multiple_of(g * group, group), group)
        flipped[:, at, :] = jnp.swapaxes(source[at], 0, 1)
        return 0

    lax.fori_loop(0, region // group, flip, 0)

    def left(g, _):
        at = pl.ds(pl.multiple_of(g * group, group), group)
        for j in range(pairs):
            products = [
                jnp.dot(
                    occupied[j], flipped[g * group + k], preferred_element_type=jnp.float32
                ).astype(jnp.bfloat16)
                for k in range(group)
            ]
            first[j, :, at, :] = jnp.swapaxes(jnp.stack(products), 0, 1)
        return 0

    lax.fori_loop(0, region // group, left, 0)
    if own is not None:
        own[...] = jnp.zeros_like(own)

    def right(g, _):
        images = []
        for k in range(few):
            l = g * few + k
            for j in range(pairs):
                image = jnp.dot(
                    virtual[j], first[j, l], preferred_element_type=jnp.float32
                ).astype(jnp.bfloat16)
                if j == own_at:
                    images.append(image)
                else:
                    outs[j - (own_at is not None and j > own_at)][l] = image
        if own is not None:
            own[...] += lax.dot_general(
                jnp.concatenate(images, axis=0),
                source[pl.ds(g * few, few)].reshape(few * region, -1),
                (((0,), (0,)), ((), ())),
                preferred_element_type=jnp.float32,
            )
        return 0

    lax.fori_loop(0, region // few, right, 0)


def transform(occupied, virtual, source, own_at):
    region, _, width = source.shape
    pairs = virtual.shape[0]
    vmem = pl.BlockSpec(memory_space=pltpu.VMEM)
    image = jax.ShapeDtypeStruct((region, region, width), jnp.bfloat16)
    shapes = [image] * pairs
    if own_at is not None:
        shapes[own_at] = jax.ShapeDtypeStruct((width, width), jnp.float32)
    return pl.pallas_call(
        functools.partial(transform_kernel, own_at),
        out_shape=shapes,
        in_specs=[vmem] * 3,
        out_specs=[vmem] * pairs,
        scratch_shapes=[
            pltpu.VMEM((region, region, width), jnp.bfloat16),
            pltpu.VMEM((pairs, region, region, width), jnp.bfloat16),
        ],
        compiler_params=pltpu.CompilerParams(vmem_limit_bytes=40 * 2**20),
        cost_estimate=pl.CostEstimate(
            flops=12 * pairs * region**3 * width, bytes_accessed=8 * 2**20, transcendentals=0
        ),
        name="transform",
    )(occupied, virtual, source)


def contract_kernel(pieces, *refs):
    down, up = refs[:2]
    parts = refs[2 : 2 + pieces]
    chi_down, chi_up, held, sem = refs[2 + pieces :]
    region = held.shape[0]

    quarter = region // 4

    def move(source, start, to, slot):
        return pltpu.make_async_copy(
            source.at[pl.ds(start, quarter)], held.at[pl.ds(to * quarter, quarter)], sem.at[slot]
        )

    def bring_whole():
        for i in range(4):
            move(parts[0], i * quarter, i, i).start()

    if pieces == 1:
        bring_whole()
    else:
        t = lax.axis_index("tau")
        odd = lax.axis_index("blk") % 2
        pl.when(odd == 0)(bring_whole)

        @pl.when(odd == 1)
        def _():
            for plane in range(2):

                @pl.when(t == plane)
                def _():
                    first, last = (parts[1], parts[3]) if plane == 0 else (parts[3], parts[1])
                    move(first, 0, 0, 0).start()
                    move(parts[2], 0, 1, 1).start()
                    move(parts[2], quarter, 2, 2).start()
                    move(last, 0, 3, 3).start()

    chi_down[...] = jnp.zeros_like(chi_down)
    chi_up[...] = jnp.zeros_like(chi_up)
    width = held.shape[2]
    rows = 8

    def body(g, _):
        def flat(ref):
            return ref[pl.ds(g * rows, rows)].reshape(rows * region, width)

        partner = flat(held)
        dims = (((0,), (0,)), ((), ()))
        chi_down[...] += lax.dot_general(partner, flat(down), dims, preferred_element_type=jnp.float32)
        chi_up[...] += lax.dot_general(flat(up), partner, dims, preferred_element_type=jnp.float32)
        return 0

    for i in range(4):
        move(parts[0], i * quarter, i, i).wait()
        lax.fori_loop(i * quarter // rows, (i + 1) * quarter // rows, body, 0)


def contract(down, up, parts):
    region, _, width = down.shape
    vmem = pl.BlockSpec(memory_space=pltpu.VMEM)
    anywhere = pl.BlockSpec(memory_space=pl.ANY)
    chi = jax.ShapeDtypeStruct((width, width), jnp.float32)
    return pl.pallas_call(
        functools.partial(contract_kernel, len(parts)),
        out_shape=(chi, chi),
        in_specs=[vmem] * 2 + [anywhere] * len(parts),
        out_specs=(vmem, vmem),
        scratch_shapes=[pltpu.VMEM((region, region, width), jnp.bfloat16), pltpu.SemaphoreType.DMA((4,))],
        compiler_params=pltpu.CompilerParams(vmem_limit_bytes=32 * 2**20),
        cost_estimate=pl.CostEstimate(
            flops=4 * region**2 * width**2, bytes_accessed=12 * 2**20, transcendentals=0
        ),
        name="contract",
    )(down, up, *parts)


def exchange(chi, weights, step):
    taus = lax.axis_size("tau")
    blks = lax.axis_size("blk")
    t = lax.axis_index("tau")
    pieces = []
    for shift in range(taus):
        target = lax.rem(t + shift, taus)
        piece = lax.dynamic_index_in_dim(weights, target, 0, keepdims=False) * chi
        if shift or step:
            perm = [
                (i * blks + j, ((i + shift) % taus) * blks + (j + step) % blks)
                for i in range(taus)
                for j in range(blks)
            ]
            piece = lax.ppermute(piece, ("tau", "blk"), perm)
        pieces.append(piece)
    return pieces


def pull_ahead(value):
    taus = lax.axis_size("tau")
    blks = lax.axis_size("blk")
    rows = value.shape[0]
    if taus != 2 or blks % 2 or rows % 4:
        return [lax.ppermute(value, "blk", [(i, (i - 1) % blks) for i in range(blks)])]
    quarter = rows // 4
    evens = [(i, (i - 1) % blks) for i in range(0, blks, 2)]
    odds = [(i, i - 1) for i in range(1, blks, 2)]
    start = lax.axis_index("tau") * (rows - quarter)
    end = lax.ppermute(lax.dynamic_slice_in_dim(value, start, quarter, 0), "blk", evens)
    middle = lax.ppermute(value[quarter : rows - quarter], "blk", evens)
    return [lax.ppermute(value, "blk", odds), end, middle]


def swap_planes(end):
    blks = lax.axis_size("blk")
    pairs = [(i * blks + j, (1 - i) * blks + j) for i in range(2) for j in range(1, blks, 2)]
    return lax.ppermute(end, ("tau", "blk"), pairs)


def local(three_center, green_blocks, block_owner, block_slot, fold_weights):
    source = three_center[0]
    devices = lax.axis_size("blk")
    per_slot = NS * NS
    slots, length = green_blocks.shape[1:]
    ids = block_owner * slots + block_slot
    asked = jnp.concatenate([block_owner[:per_slot], block_slot[:per_slot]]).astype(jnp.bfloat16)
    riders = jnp.broadcast_to(jnp.pad(asked, (0, LANES - 2 * per_slot)), (slots, LANES))
    table = lax.all_gather(
        jnp.concatenate([green_blocks[0], riders], axis=1), "blk", axis=0, tiled=True
    )
    table, sent = lax.optimization_barrier((table, source))
    ahead = lax.rem(lax.axis_index("blk") + 1, devices)
    asked = lax.dynamic_slice(table, (ahead * slots, length), (1, 2 * per_slot))[0].astype(jnp.int32)
    next_ids = asked[:per_slot] * slots + asked[per_slot:]
    used = jnp.concatenate([next_ids, ids[per_slot:]])
    parts = pull_ahead(sent)
    fetched = table.at[used].get(mode="promise_in_bounds")[:, :length]
    occupied, virtual = green_pairs(fetched)
    weights = fold_weights[:, 0] * -2.0
    (down,) = transform(occupied[:1].swapaxes(1, 2), virtual[:1].swapaxes(1, 2), source, None)
    occupied, virtual = occupied[1:], virtual[1:]
    if len(parts) > 1:
        down, occupied, virtual, parts[1] = lax.optimization_barrier((down, occupied, virtual, parts[1]))
        parts.append(swap_planes(parts[1]))
    chi_own, up = transform(occupied, virtual, source, 0)
    own = exchange(chi_own, weights, 0)
    chi_down, chi_up = contract(down, up, parts)
    chi_down, chi_up, own = lax.optimization_barrier((chi_down, chi_up, own))
    down = exchange(chi_down, weights, 1)
    up = exchange(chi_up, weights, 0)
    return jnp.concatenate([sum(down), sum(own), sum(up)], axis=1)[None]


def solution(mesh):
    return jax.shard_map(
        local,
        mesh=mesh,
        in_specs=(
            P("blk", None, None, None),
            P("tau", "blk", None),
            P("blk"),
            P("blk"),
            P(None, "tau"),
        ),
        out_specs=P("tau", "blk", None),
        check_vma=False,
    )
```
